32 devices in a mesh: groups: 2 (over y), expert: 4 (over z), tensor: 2 (over x), dp: 2 (over core).
Axes of the slice: x: 2, y: 2, z: 4, core: 2. Of those that a mesh axis runs over, the one named last changes fastest.
Arguments:
- tokens: bfloat16 [1536, 7168], P(('groups', 'expert', 'dp'), 'tensor'), parts along dimension 0, may hold values from -6 to 6
- route_weight: bfloat16 [1536], P(('groups', 'expert', 'dp')), parts along dimension 0, may hold values from 0.25 to 1
- block_start: int32 [16, 2], P(('groups', 'expert', 'dp')), parts along dimension 0, may hold values from 0 to 96, as said below
- block_count: int32 [16, 2], P(('groups', 'expert', 'dp')), parts along dimension 0, may hold values from 0 to 64
- spill_rows: int32 [16, 2, 32], P(('groups', 'expert', 'dp')), parts along dimension 0, may hold values from 0 to 95
- spill_count: int32 [16, 2], P(('groups', 'expert', 'dp')), parts along dimension 0, may hold values from 0 to 32
- in_weights: bfloat16 [2, 7168, 2, 2048], P(None, 'expert', None, ('tensor', 'dp')), may hold values from -0.0625 to 0.0625
- out_weights: bfloat16 [2, 2048, 7168], P(None, ('tensor', 'dp'), 'expert'), may hold values from -0.125 to 0.125
Outputs:
- layer_out: bfloat16 [1536, 7168], P(('groups', 'expert', 'dp'), 'tensor'), parts along dimension 0
The draws below stay inside these ranges and needn't reach their ends.
There are 2 independent parts, one for each index of `groups`. The reference program is written for one: setup_inputs(seed, part) draws one part's arguments, and reference() takes and returns one part's arrays. A program takes and returns all parts, laid end to end along the dimension named above; an argument that names none is the same for every part. Nothing has to cross between parts.
Inputs may be any that keep to these rules, and one draw needn't show every extreme that they name: In every shard the rows are ordered by first-choice expert: expert 0's block starts at row 0, expert 1's at block_start; block_count is that block's size capped at 64. The rows of a block past 64 are the first spill_count entries of the other expert's spill_rows, in some order; the other entries are 0. Each token is served by exactly one live slot. Some shard of every draw puts all 96 rows into expert 0's block.
All inputs are finite; a program needn't handle non-finite values.
Results may differ from the reference program's by a relative error of at most 0.009.
Values may be sent and summed in bfloat16 or wider, within the bound.
A program may use at most 192 MiB of HBM per device.

```python
import jax
import jax.numpy as jnp
from jax import lax

D = 7168
FF = 2048
EXPERTS = 2
TOK_DEV = 96
SPILL = 32
CAP = 64
SHARDS = 8
TOKENS = 768
N_TENSOR = 2
N_DP = 2


def routing_plan(key):
    keys = jax.random.split(key, 4)
    heavy = jax.random.randint(keys[0], (SHARDS,), 0, 2)
    loaded = jax.random.randint(keys[1], (SHARDS,), CAP, TOK_DEV + 1)
    forced = jax.random.randint(keys[2], (), 0, SHARDS)
    chosen = jnp.arange(SHARDS) == forced
    heavy = jnp.where(chosen, 0, heavy)
    loaded = jnp.where(chosen, TOK_DEV, loaded)
    first_size = jnp.where(heavy == 0, loaded, TOK_DEV - loaded)
    starts = jnp.stack([jnp.zeros_like(first_size), first_size], axis=1)
    counts = jnp.stack([jnp.minimum(first_size, CAP), jnp.minimum(TOK_DEV - first_size, CAP)], axis=1)
    dropped = loaded - CAP
    heavy_start = jnp.where(heavy == 0, 0, first_size)
    rotate = jax.random.randint(keys[3], (SHARDS, 1), 0, SPILL)
    positions = jnp.arange(SPILL)[None, :]
    listed = heavy_start[:, None] + CAP + (positions + rotate) % jnp.maximum(dropped, 1)[:, None]
    listed = jnp.where(positions < dropped[:, None], listed, 0)
    light = 1 - heavy
    picks = jnp.arange(2)[None, :] == light[:, None]
    spills = jnp.where(picks[:, :, None], listed[:, None, :], 0)
    spill_counts = jnp.where(picks, dropped[:, None], 0)
    return (starts.astype(jnp.int32), counts.astype(jnp.int32), spills.astype(jnp.int32), spill_counts.astype(jnp.int32))


def draw_block_start(key, part):
    return routing_plan(key)[0]


def draw_block_count(key, part):
    return routing_plan(key)[1]


def draw_spill_rows(key, part):
    return routing_plan(key)[2]


def draw_spill_count(key, part):
    return routing_plan(key)[3]


def block_scale(key, dims, cuts, low, top_value):
    level = 1.0
    for dim, parts in cuts:
        heights = jax.random.uniform(jax.random.fold_in(jax.random.fold_in(key, 6), dim), (parts,), jnp.float32, low / len(cuts), top_value / len(cuts))
        level = level * jnp.repeat(jnp.exp(heights), dims[dim] // parts).reshape((-1,) + (1,) * (len(dims) - 1 - dim))
    return level


def noise(rng, shape, width, bound, pieces=(), held_as=jnp.bfloat16):
    values = jax.random.normal(rng, shape, jnp.float32) * width
    if len(pieces) > 0:
        values = block_scale(rng, shape, pieces, -0.22, 0.18) * values
    return jnp.clip(values, min=-bound, max=bound).astype(held_as)


def setup_inputs(seed: int = 0, part: int = 0) -> dict:
    key_of = jax.random.split(jax.random.key(seed), 9)
    part_keys = jax.random.split(jax.random.fold_in(key_of[8], part), 9)
    tokens = noise(part_keys[0], (TOKENS, D), 1.0, 6.0, ((0, 8), (1, 2)))
    route_weight = jnp.clip(0.25 + 0.75 * jax.random.uniform(part_keys[1], (TOKENS,), jnp.float32) ** block_scale(part_keys[1], (TOKENS,), ((0, 8),), -0.2, 0.2), 0.25, 1.0).astype(jnp.bfloat16)
    block_start = draw_block_start(jax.random.fold_in(jax.random.fold_in(key_of[8], part), 71), part)
    block_count = draw_block_count(jax.random.fold_in(jax.random.fold_in(key_of[8], part), 71), part)
    spill_rows = draw_spill_rows(jax.random.fold_in(jax.random.fold_in(key_of[8], part), 71), part)
    spill_count = draw_spill_count(jax.random.fold_in(jax.random.fold_in(key_of[8], part), 71), part)
    in_weights = noise(key_of[6], (EXPERTS, D, 2, FF), D ** -0.5, 0.0625, ((1, 4), (3, 4)))
    out_weights = noise(key_of[7], (EXPERTS, FF, D), FF ** -0.5, 0.125, ((1, 4), (2, 4)))
    return {"tokens": tokens, "route_weight": route_weight, "block_start": block_start, "block_count": block_count, "spill_rows": spill_rows, "spill_count": spill_count, "in_weights": in_weights, "out_weights": out_weights}


def slot_plan(starts, counts, spills, spill_counts, rows_each):
    overflow = spills.shape[-1]
    capacity = rows_each - overflow
    first_pos = jnp.arange(capacity, dtype=jnp.int32)
    spill_pos = jnp.arange(overflow, dtype=jnp.int32)
    block_rows = starts[..., None].astype(jnp.int32) + first_pos
    slot_rows = jnp.clip(jnp.concatenate([block_rows, spills.astype(jnp.int32)], axis=-1), 0, rows_each - 1)
    slot_live = jnp.concatenate([first_pos < counts[..., None], spill_pos < spill_counts[..., None]], axis=-1)
    return slot_rows.astype(jnp.int32), slot_live


def reference(tokens, route_weight, block_start, block_count, spill_rows, spill_count, in_weights, out_weights):
    slices = N_TENSOR * N_DP
    slice_width = FF // slices
    shard_tokens = tokens.reshape(SHARDS, TOK_DEV, D)
    shard_weights = route_weight.reshape(SHARDS, TOK_DEV)
    down_wide = out_weights.astype(jnp.float32).reshape(EXPERTS, slices, slice_width, D)

    def one_shard(operands):
        features, weighting, starts, counts, spills, spill_counts = operands
        slot_rows, slot_live = slot_plan(starts, counts, spills, spill_counts, TOK_DEV)
        placed_list = []
        for expert in range(EXPERTS):
            rows = slot_rows[expert]
            picked = features[rows]
            gate_part = jnp.dot(picked, in_weights[expert, :, 0, :], preferred_element_type=jnp.float32)
            up_part = jnp.dot(picked, in_weights[expert, :, 1, :], preferred_element_type=jnp.float32)
            scaling = weighting[rows].astype(jnp.float32) * slot_live[expert].astype(jnp.float32)
            hidden_act = (jax.nn.silu(gate_part) * up_part * scaling[:, None]).astype(jnp.bfloat16)
            placed = jnp.zeros((TOK_DEV, FF), jnp.float32).at[rows].add(hidden_act.astype(jnp.float32))
            placed_list.append(placed)
        stacked = jnp.stack(placed_list).reshape(EXPERTS, TOK_DEV, slices, slice_width)
        partial_value = jnp.einsum("erkh,ekhd->krd", stacked, down_wide)
        rounded = lax.optimization_barrier(partial_value.astype(jnp.bfloat16)).astype(jnp.float32)
        return jnp.sum(rounded, axis=0).astype(jnp.bfloat16)

    result = lax.map(one_shard, (shard_tokens, shard_weights, block_start, block_count, spill_rows, spill_count))
    return result.reshape(TOKENS, D)
```

```python
import jax
import jax.numpy as jnp
from jax import lax
from jax.sharding import PartitionSpec as P


def token_scales(route_weight, starts, counts, spills, spill_counts):
    rows_each = route_weight.shape[0]
    overflow = spills.shape[-1]
    capacity = rows_each - overflow
    first_pos = jnp.arange(capacity, dtype=jnp.int32)
    spill_pos = jnp.arange(overflow, dtype=jnp.int32)
    slot_rows = jnp.clip(
        jnp.concatenate([starts[:, None] + first_pos, spills], axis=-1), 0, rows_each - 1
    )
    slot_live = jnp.concatenate(
        [first_pos < counts[:, None], spill_pos < spill_counts[:, None]], axis=-1
    )
    hits = (slot_rows[:, :, None] == jnp.arange(rows_each)) & slot_live[:, :, None]
    live = jnp.sum(hits.astype(jnp.float32), axis=1)
    return live * route_weight.astype(jnp.float32)


def local(
    tokens, route_weight, block_start, block_count, spill_rows, spill_count, in_weights, out_weights
):
    rows, cols = tokens.shape
    n_z = lax.axis_size("expert")
    n_p = lax.axis_size("dp")
    depth = in_weights.shape[1]
    half = in_weights.shape[3]
    scales = token_scales(
        route_weight, block_start[0], block_count[0], spill_rows[0], spill_count[0]
    )
    scales_all = lax.all_gather(scales, ("expert", "dp"), axis=1, tiled=True)
    wide = lax.all_gather(tokens, "tensor", axis=1, tiled=True)
    wide = wide.reshape(rows, n_z, depth).transpose(1, 0, 2)
    mine = lax.all_to_all(wide, "expert", 0, 0, tiled=True)
    x = lax.all_gather(mine, "dp", axis=1, tiled=True).reshape(n_z * n_p * rows, depth)
    total = x.shape[0]
    use = (scales_all > 0).astype(x.dtype)
    part = sum(
        jnp.einsum(
            "rk,kgh->rgh", x * use[e][:, None], in_weights[e], preferred_element_type=jnp.float32
        )
        for e in range(2)
    )
    part = part.reshape(total, 2 * half).astype(jnp.bfloat16)
    gate_up = lax.psum_scatter(part, "expert", scatter_dimension=0, tiled=True).astype(jnp.float32)
    here = lax.all_gather(scales, "dp", axis=1, tiled=True)
    weight = jnp.sum(here, axis=0)
    act = (
        jax.nn.silu(gate_up[:, :half]) * gate_up[:, half:] * weight[:, None]
    ).astype(jnp.bfloat16)
    act = lax.all_gather(act, "expert", axis=0, tiled=True)
    placed = jnp.concatenate([act * use[0][:, None], act * use[1][:, None]], axis=1)
    out = jnp.dot(
        placed,
        out_weights.reshape(2 * half, depth),
        preferred_element_type=jnp.float32,
    ).astype(jnp.bfloat16)
    out = out.reshape(n_z, n_p, rows, depth).transpose(1, 0, 2, 3)
    out = lax.psum_scatter(out, "dp", scatter_dimension=0, tiled=True)[0]
    out = lax.all_to_all(out, "expert", 0, 0, tiled=True)
    out = out.transpose(1, 0, 2).reshape(rows, n_z * depth)
    return lax.psum_scatter(out, "tensor", scatter_dimension=1, tiled=True)


def solution(mesh):
    return jax.shard_map(
        local,
        mesh=mesh,
        in_specs=(
            P(("groups", "expert", "dp"), "tensor"),
            P(("groups", "expert", "dp")),
            P(("groups", "expert", "dp"), None),
            P(("groups", "expert", "dp"), None),
            P(("groups", "expert", "dp"), None, None),
            P(("groups", "expert", "dp"), None),
            P(None, "expert", None, ("tensor", "dp")),
            P(None, ("tensor", "dp"), "expert"),
        ),
        out_specs=P(("groups", "expert", "dp"), "tensor"),
        check_vma=False,
    )
```

```python
import functools

import jax
import jax.numpy as jnp
from jax import lax
from jax.experimental import pallas as pl
from jax.experimental.pallas import tpu as pltpu
from jax.sharding import PartitionSpec as P

MESH = pl.DeviceIdType.MESH
LANES = 128


def token_scales(route_weight, starts, counts, spills, spill_counts):
    rows_each = route_weight.shape[0]
    overflow = spills.shape[-1]
    capacity = rows_each - overflow
    first_pos = jnp.arange(capacity, dtype=jnp.int32)
    spill_pos = jnp.arange(overflow, dtype=jnp.int32)
    slot_rows = jnp.clip(
        jnp.concatenate([starts[:, None] + first_pos, spills], axis=-1), 0, rows_each - 1
    )
    slot_live = jnp.concatenate(
        [first_pos < counts[:, None], spill_pos < spill_counts[:, None]], axis=-1
    )
    hits = (slot_rows[:, :, None] == jnp.arange(rows_each)) & slot_live[:, :, None]
    live = jnp.sum(hits.astype(jnp.float32), axis=1)
    return live * route_weight.astype(jnp.float32)


def kernel(
    n_t, n_z, n_r, rows, width, half,
    xs, w_in, w_out, out_ref,
    wi, wo, first, x_all, part, part_in, hid, o_both, o_sib, x_out, x_in, z_out, z_in, last,
    wsem, lsem, s0, r0, s1, r1, s2, r2, s3, r3, s4, r4, s5, r5, s6, r6, s7, r7, s8, r8, s9, r9,
):
    e = lax.axis_index("expert")
    t = lax.axis_index("tensor")
    p = lax.axis_index("dp")
    other = 1 - p
    total = 2 * n_t * rows

    load_in = pltpu.make_async_copy(w_in, wi, wsem.at[0])
    load_out = pltpu.make_async_copy(w_out, wo, wsem.at[1])
    own_piece = pltpu.make_async_copy(xs.at[t], first.at[t], lsem.at[0])
    own_piece.start()
    load_in.start()
    load_out.start()

    barrier = pltpu.get_barrier_semaphore()
    for k in range(1, n_t):
        pl.semaphore_signal(
            barrier, inc=1, device_id={"tensor": lax.rem(t + k, n_t)}, device_id_type=MESH
        )
    for k in range(1, n_z):
        pl.semaphore_signal(
            barrier, inc=1, device_id={"expert": lax.rem(e + k, n_z)}, device_id_type=MESH
        )
    pl.semaphore_signal(barrier, inc=1, device_id={"dp": other}, device_id_type=MESH)
    pl.semaphore_wait(barrier, n_t + n_z - 1)

    def remote(src, dst, send, recv, **where):
        return pltpu.make_async_remote_copy(
            src_ref=src,
            dst_ref=dst,
            send_sem=send,
            recv_sem=recv,
            device_id=where,
            device_id_type=MESH,
        )

    def spread(to, j, came):
        return remote(
            xs.at[to, j], first.at[came, j], s0.at[to, j], r0.at[came, j], tensor=to
        )

    def across(block, to, came):
        return remote(
            first.at[block // n_r, lax.rem(block, n_r)],
            x_all.at[came, p, t],
            s1.at[to],
            r1.at[came],
            expert=to,
        )

    def widen(block, to, came):
        return remote(
            x_all.at[block, p, came],
            x_all.at[block, p, came],
            s2.at[block, to],
            r2.at[block, came],
            tensor=to,
        )

    def pair(block, core):
        return remote(
            x_all.at[block, core], x_all.at[block, core], s3.at[block], r3.at[block], dp=other
        )

    def partial(block, came):
        return remote(part.at[block], part_in.at[came], s4.at[block], r4.at[came], expert=block)

    def hidden(to, came):
        return remote(hid.at[came], hid.at[came], s5.at[to], r5.at[came], expert=to)

    def sibling(block):
        return remote(
            o_both.at[block, other], o_sib.at[block], s6.at[block], r6.at[block], dp=other
        )

    def reduce_x(block, to, came):
        return remote(
            x_out.at[block, to], x_in.at[block, came], s7.at[block, to], r7.at[block, came],
            tensor=to,
        )

    def deliver(to, came):
        return remote(z_out.at[to], z_in.at[came], s8.at[to], r8.at[came], expert=to)

    def finish(block, to, j, came):
        return remote(
            z_in.at[block], last.at[j, came], s9.at[block], r9.at[j, came], tensor=to
        )

    for j in range(n_r):
        for k in range(1, n_t):
            spread(lax.rem(t + k, n_t), j, t).start()
    own_piece.wait()
    for k in range(n_t):
        ts = lax.rem(t + k, n_t)
        for j in range(n_r):
            block = ts * n_r + j
            if k > 0:
                spread(ts, j, ts).wait_recv()

            @pl.when(block != e)
            def _():
                across(block, block, e).start()

            @pl.when(block == e)
            def _():
                pltpu.make_async_copy(first.at[ts, j], x_all.at[e, p, t], lsem.at[1]).start()

    def stage_a(k):
        es = lax.rem(e + k, n_z)
        if k == 0:
            pltpu.make_async_copy(first.at[0, 0], x_all.at[e, p, t], lsem.at[1]).wait()
        else:
            across(es, es, es).wait_recv()
        for i in range(1, n_t):
            widen(es, lax.rem(t + i, n_t), t).start()

    def stage_b(k):
        es = lax.rem(e + k, n_z)
        for i in range(1, n_t):
            ts = lax.rem(t + i, n_t)
            widen(es, ts, ts).wait_recv()
        pair(es, p).start()

    def signs(es):
        meta = x_all[es, :, :, :, :LANES].reshape(total, LANES)
        return meta.astype(jnp.float32)[:, :1]

    tile = min(half, 256)
    tiles = half // tile

    def stage_c(k):
        es = lax.rem(e + k, n_z)
        pair(es, other).wait_recv()
        second = signs(es) < 0

        def step(i, carry):
            g = i // tiles
            cols = pl.ds(pl.multiple_of(lax.rem(i, tiles) * tile, tile), tile)
            x = x_all[es, :, :, :, LANES:].reshape(total, width)
            zero = jnp.dot(x, wi[0, g, :, cols], preferred_element_type=jnp.float32)
            one = jnp.dot(x, wi[1, g, :, cols], preferred_element_type=jnp.float32)
            value = jnp.where(second, one, zero).astype(jnp.bfloat16)
            if k == 0:
                part_in[e, g, :, cols] = value
            else:
                part[es, g, :, cols] = value
            return carry

        lax.fori_loop(0, 2 * tiles, step, 0)
        if k > 0:
            partial(es, e).start()

    for step in range(n_z + 2):
        if step < n_z:
            stage_a(step)
        if 0 <= step - 1 < n_z:
            stage_b(step - 1)
        if step - 1 == 0:
            load_in.wait()
        if 0 <= step - 2 < n_z:
            stage_c(step - 2)

    for k in range(1, n_z):
        es = lax.rem(e + k, n_z)
        partial(es, es).wait_recv()
    gate = jnp.zeros((total, half), jnp.float32)
    up = jnp.zeros((total, half), jnp.float32)
    for k in range(n_z):
        gate = gate + part_in[k, 0].astype(jnp.float32)
        up = up + part_in[k, 1].astype(jnp.float32)
    act = gate / (1.0 + jnp.exp(-gate)) * up * jnp.abs(signs(e))
    hid[e] = act.astype(jnp.bfloat16)
    for k in range(1, n_z):
        hidden(lax.rem(e + k, n_z), e).start()

    load_out.wait()
    wide = 256 if width % 256 == 0 else width

    def stage_d(k):
        es = lax.rem(e + k, n_z)
        if k > 0:
            hidden(es, es).wait_recv()
        second = signs(es) < 0
        h = hid[es].astype(jnp.float32)
        h0 = jnp.where(second, 0.0, h).astype(jnp.bfloat16)
        h1 = jnp.where(second, h, 0.0).astype(jnp.bfloat16)

        def column(i):
            if wide == width:
                cols = slice(None)
            else:
                cols = pl.ds(pl.multiple_of(i * wide, wide), wide)
            value = jnp.dot(h0, wo[0, :, cols], preferred_element_type=jnp.float32)
            value = value + jnp.dot(h1, wo[1, :, cols], preferred_element_type=jnp.float32)
            value = value.astype(jnp.bfloat16).reshape(2, n_t, rows, wide)
            o_both[es, :, :, :, cols] = value

        if wide == width:
            column(0)
        else:
            lax.fori_loop(0, width // wide, lambda i, c: (column(i), c)[1], 0)
        sibling(es).start()

    def stage_e(k):
        es = lax.rem(e + k, n_z)
        sibling(es).wait_recv()
        both = o_both[es, p].astype(jnp.float32) + o_sib[es].astype(jnp.float32)
        x_out[es] = both.astype(jnp.bfloat16)
        for i in range(1, n_t):
            reduce_x(es, lax.rem(t + i, n_t), t).start()

    def stage_f(k):
        es = lax.rem(e + k, n_z)
        value = x_out[es, t].astype(jnp.float32)
        for i in range(1, n_t):
            ts = lax.rem(t + i, n_t)
            reduce_x(es, ts, ts).wait_recv()
            value = value + x_in[es, ts].astype(jnp.float32)
        if k == 0:
            z_in[e] = value.astype(jnp.bfloat16)
        else:
            z_out[es] = value.astype(jnp.bfloat16)
            deliver(es, e).start()

    for step in range(n_z + 2):
        if step < n_z:
            stage_d(step)
        if 0 <= step - 1 < n_z:
            stage_e(step - 1)
        if 0 <= step - 2 < n_z:
            stage_f(step - 2)

    for k in range(n_z):
        es = lax.rem(e + k, n_z)
        if k > 0:
            deliver(es, es).wait_recv()
        owner = es // n_r
        j = lax.rem(es, n_r)

        @pl.when(owner != t)
        def _():
            finish(es, owner, j, t).start()

        @pl.when(owner == t)
        def _():
            last[j, t] = z_in[es]

    for k in range(1, n_t):
        ts = lax.rem(t + k, n_t)
        for j in range(n_r):
            finish(0, ts, j, ts).wait_recv()
    out_ref[...] = last[...]

    for k in range(1, n_t):
        ts = lax.rem(t + k, n_t)
        for j in range(n_r):
            spread(ts, j, t).wait_send()
            finish(ts * n_r + j, ts, j, t).wait_send()
        for b in range(n_z):
            widen(b, ts, t).wait_send()
            reduce_x(b, ts, t).wait_send()
    for k in range(1, n_z):
        es = lax.rem(e + k, n_z)
        across(es, es, e).wait_send()
        partial(es, e).wait_send()
        hidden(es, e).wait_send()
        deliver(es, e).wait_send()
    for b in range(n_z):
        pair(b, p).wait_send()
        sibling(b).wait_send()


def local(
    tokens, route_weight, block_start, block_count, spill_rows, spill_count, in_weights, out_weights
):
    rows_each, cols = tokens.shape
    n_z = lax.axis_size("expert")
    n_t = lax.axis_size("tensor")
    n_r = n_z // n_t
    width = in_weights.shape[1]
    half = in_weights.shape[3]
    scales = token_scales(
        route_weight, block_start[0], block_count[0], spill_rows[0], spill_count[0]
    )
    signed = (scales[0] - scales[1]).astype(jnp.bfloat16)
    rows = -(-rows_each // (16 * n_t)) * 16
    extra = rows * n_t - rows_each
    if extra:
        tokens = jnp.pad(tokens, ((0, extra), (0, 0)))
        signed = jnp.pad(signed, (0, extra))
    meta = jnp.broadcast_to(signed.reshape(n_t, 1, rows, 1), (n_t, n_r, rows, LANES))
    blocks = tokens.reshape(n_t, rows, n_r, width).transpose(0, 2, 1, 3)
    xs = jnp.concatenate([meta, blocks], axis=-1)
    w_in = in_weights.transpose(0, 2, 1, 3)

    total = 2 * n_t * rows
    long = width + LANES
    b16 = jnp.bfloat16
    dma = pltpu.SemaphoreType.DMA
    sems = [
        dma((2,)), dma((2,)),
        dma((n_t, n_r)), dma((n_t, n_r)),
        dma((n_z,)), dma((n_z,)),
        dma((n_z, n_t)), dma((n_z, n_t)),
        dma((n_z,)), dma((n_z,)),
        dma((n_z,)), dma((n_z,)),
        dma((n_z,)), dma((n_z,)),
        dma((n_z,)), dma((n_z,)),
        dma((n_z, n_t)), dma((n_z, n_t)),
        dma((n_z,)), dma((n_z,)),
        dma((n_z,)), dma((n_r, n_t)),
    ]
    vmem = pltpu.VMEM
    out = pl.pallas_call(
        functools.partial(kernel, n_t, n_z, n_r, rows, width, half),
        out_shape=jax.ShapeDtypeStruct((n_r, n_t, rows, width), b16),
        in_specs=[
            pl.BlockSpec(memory_space=pltpu.VMEM),
            pl.BlockSpec(memory_space=pl.ANY),
            pl.BlockSpec(memory_space=pl.ANY),
        ],
        out_specs=pl.BlockSpec(memory_space=pltpu.VMEM),
        scratch_shapes=[
            vmem(w_in.shape, b16),
            vmem(out_weights.shape, b16),
            vmem((n_t, n_r, rows, long), b16),
            vmem((n_z, 2, n_t, rows, long), b16),
            vmem((n_z, 2, total, half), b16),
            vmem((n_z, 2, total, half), b16),
            vmem((n_z, total, half), b16),
            vmem((n_z, 2, n_t, rows, width), b16),
            vmem((n_z, n_t, rows, width), b16),
            vmem((n_z, n_t, rows, width), b16),
            vmem((n_z, n_t, rows, width), b16),
            vmem((n_z, rows, width), b16),
            vmem((n_z, rows, width), b16),
            vmem((n_r, n_t, rows, width), b16),
        ] + sems,
        compiler_params=pltpu.CompilerParams(
            collective_id=0, has_side_effects=True, vmem_limit_bytes=56 * 1024 * 1024
        ),
    )(xs, w_in, out_weights)
    out = out.transpose(1, 2, 0, 3).reshape(n_t * rows, cols)
    return out[:rows_each]


def solution(mesh):
    return jax.shard_map(
        local,
        mesh=mesh,
        in_specs=(
            P(("groups", "expert", "dp"), "tensor"),
            P(("groups", "expert", "dp")),
            P(("groups", "expert", "dp"), None),
            P(("groups", "expert", "dp"), None),
            P(("groups", "expert", "dp"), None, None),
            P(("groups", "expert", "dp"), None),
            P(None, "expert", None, ("tensor", "dp")),
            P(None, ("tensor", "dp"), "expert"),
        ),
        out_specs=P(("groups", "expert", "dp"), "tensor"),
        check_vma=False,
    )
```

```python
import functools

import jax
import jax.numpy as jnp
from jax import lax
from jax.experimental import pallas as pl
from jax.experimental.pallas import tpu as pltpu
from jax.sharding import PartitionSpec as P

MESH = pl.DeviceIdType.MESH
LANES = 128


def token_scales(route_weight, starts, counts, spills, spill_counts):
    rows_each = route_weight.shape[0]
    overflow = spills.shape[-1]
    capacity = rows_each - overflow
    first_pos = jnp.arange(capacity, dtype=jnp.int32)
    spill_pos = jnp.arange(overflow, dtype=jnp.int32)
    slot_rows = jnp.clip(
        jnp.concatenate([starts[:, None] + first_pos, spills], axis=-1), 0, rows_each - 1
    )
    slot_live = jnp.concatenate(
        [first_pos < counts[:, None], spill_pos < spill_counts[:, None]], axis=-1
    )
    hits = (slot_rows[:, :, None] == jnp.arange(rows_each)) & slot_live[:, :, None]
    live = jnp.sum(hits.astype(jnp.float32), axis=1)
    return live * route_weight.astype(jnp.float32)


def kernel(
    n_t, n_z, n_r, rows, width, half,
    xs, w_in, w_out, out_ref,
    wi, wo, first, x_all, part, run_out, run_in, hid, o_both, o_sib, x_out, x_in, z_out, z_in, last,
    wsem, lsem, s0, r0, s1, r1, s2, r2, s3, r3, s4, r4, s5, r5, s6, r6, s7, r7, s8, r8, s9, r9,
):
    e = lax.axis_index("expert")
    t = lax.axis_index("tensor")
    p = lax.axis_index("dp")
    other = 1 - p
    total = 2 * n_t * rows

    load_in = pltpu.make_async_copy(w_in, wi, wsem.at[0])
    load_out = pltpu.make_async_copy(w_out, wo, wsem.at[1])
    own_piece = pltpu.make_async_copy(xs.at[t], first.at[t], lsem.at[0])
    own_piece.start()
    load_in.start()
    load_out.start()

    barrier = pltpu.get_barrier_semaphore()
    for k in range(1, n_t):
        pl.semaphore_signal(
            barrier, inc=1, device_id={"tensor": lax.rem(t + k, n_t)}, device_id_type=MESH
        )
    for k in range(1, n_z):
        pl.semaphore_signal(
            barrier, inc=1, device_id={"expert": lax.rem(e + k, n_z)}, device_id_type=MESH
        )
    pl.semaphore_signal(barrier, inc=1, device_id={"dp": other}, device_id_type=MESH)
    pl.semaphore_wait(barrier, n_t + n_z - 1)

    def remote(src, dst, send, recv, **where):
        return pltpu.make_async_remote_copy(
            src_ref=src,
            dst_ref=dst,
            send_sem=send,
            recv_sem=recv,
            device_id=where,
            device_id_type=MESH,
        )

    def spread(to, j, came):
        return remote(
            xs.at[to, j], first.at[came, j], s0.at[to, j], r0.at[came, j], tensor=to
        )

    def across(block, to, came):
        return remote(
            first.at[block // n_r, lax.rem(block, n_r)],
            x_all.at[came, p, t],
            s1.at[to],
            r1.at[came],
            expert=to,
        )

    def widen(block, to, came):
        return remote(
            x_all.at[block, p, came],
            x_all.at[block, p, came],
            s2.at[block, to],
            r2.at[block, came],
            tensor=to,
        )

    def pair(block, core):
        return remote(
            x_all.at[block, core], x_all.at[block, core], s3.at[block], r3.at[block], dp=other
        )

    def partial(block, c, to):
        return remote(
            run_out.at[block, c], run_in.at[block, c], s4.at[block, c], r4.at[block, c], expert=to
        )

    def hidden(block, c, to):
        return remote(
            hid.at[block, c], hid.at[block, c], s5.at[block, c], r5.at[block, c], expert=to
        )

    last_z = n_z - 1
    order = []
    for i in range(n_z // 2):
        order += [(last_z - i, True), (i, False)]
    prev_z = jnp.maximum(e - 1, 0)
    next_z = jnp.minimum(e + 1, last_z)

    def sibling(block):
        return remote(
            o_both.at[block, other], o_sib.at[block], s6.at[block], r6.at[block], dp=other
        )

    def reduce_x(block, to, came):
        return remote(
            x_out.at[block, to], x_in.at[block, came], s7.at[block, to], r7.at[block, came],
            tensor=to,
        )

    def deliver(to, came):
        return remote(z_out.at[to], z_in.at[came], s8.at[to], r8.at[came], expert=to)

    def finish(block, to, j, came):
        return remote(
            z_in.at[block], last.at[j, came], s9.at[block], r9.at[j, came], tensor=to
        )

    for j in range(n_r):
        for k in range(1, n_t):
            spread(lax.rem(t + k, n_t), j, t).start()
    own_piece.wait()
    for k in range(n_t):
        ts = lax.rem(t + k, n_t)
        for j in range(n_r):
            block = ts * n_r + j
            if k > 0:
                spread(ts, j, ts).wait_recv()

            @pl.when(block != e)
            def _():
                across(block, block, e).start()

            @pl.when(block == e)
            def _():
                pltpu.make_async_copy(first.at[ts, j], x_all.at[e, p, t], lsem.at[1]).start()

    def stage_a(k):
        es = lax.rem(e + k, n_z)
        if k == 0:
            pltpu.make_async_copy(first.at[0, 0], x_all.at[e, p, t], lsem.at[1]).wait()
        else:
            across(es, es, es).wait_recv()
        for i in range(1, n_t):
            widen(es, lax.rem(t + i, n_t), t).start()

    def stage_b(k):
        es = lax.rem(e + k, n_z)
        for i in range(1, n_t):
            ts = lax.rem(t + i, n_t)
            widen(es, ts, ts).wait_recv()
        pair(es, p).start()

    def signs(es):
        meta = x_all[es, :, :, :, :LANES].reshape(total, LANES)
        return meta.astype(jnp.float32)[:, :1]

    tile = min(half, 256)
    tiles = half // tile

    def stage_c(k):
        es = lax.rem(e + k, n_z)
        pair(es, other).wait_recv()
        second = signs(es) < 0

        def step(i, carry):
            g = i // tiles
            cols = pl.ds(pl.multiple_of(lax.rem(i, tiles) * tile, tile), tile)
            x = x_all[es, :, :, :, LANES:].reshape(total, width)
            zero = jnp.dot(x, wi[0, g, :, cols], preferred_element_type=jnp.float32)
            one = jnp.dot(x, wi[1, g, :, cols], preferred_element_type=jnp.float32)
            part[es, i] = jnp.where(second, one, zero)
            return carry

        lax.fori_loop(0, 2 * tiles, step, 0)

        @pl.when((e == last_z) & (es >= n_z // 2))
        def _():
            for c in range(2 * tiles):
                run_out[es, c] = part[es, c].astype(jnp.bfloat16)
                partial(es, c, prev_z).start()

        @pl.when((e == 0) & (es < n_z // 2))
        def _():
            for c in range(2 * tiles):
                run_out[es, c] = part[es, c].astype(jnp.bfloat16)
                partial(es, c, next_z).start()

    for step in range(n_z + 2):
        if step < n_z:
            stage_a(step)
        if 0 <= step - 1 < n_z:
            stage_b(step - 1)
        if step - 1 == 0:
            load_in.wait()
        if 0 <= step - 2 < n_z:
            stage_c(step - 2)

    def combine(b, down):
        begin, end = (last_z, 0) if down else (0, last_z)
        to, back = (prev_z, next_z) if down else (next_z, prev_z)

        @pl.when((e != begin) & (e != end))
        def _():
            for c in range(2 * tiles):
                partial(b, c, back).wait_recv()
                value = part[b, c] + run_in[b, c].astype(jnp.float32)
                run_out[b, c] = value.astype(jnp.bfloat16)
                partial(b, c, to).start()

        @pl.when(e == end)
        def _():
            for c in range(2 * tiles):
                partial(b, c, back).wait_recv()
            scale = jnp.abs(signs(b))
            for c in range(tiles):
                gate = part[b, c] + run_in[b, c].astype(jnp.float32)
                up = part[b, tiles + c] + run_in[b, tiles + c].astype(jnp.float32)
                act = gate / (1.0 + jnp.exp(-gate)) * up * scale
                hid[b, c] = act.astype(jnp.bfloat16)
                hidden(b, c, back).start()

    def relay(b, down):
        begin, end = (last_z, 0) if down else (0, last_z)
        to, back = (prev_z, next_z) if down else (next_z, prev_z)
        for c in range(tiles):

            @pl.when(e != end)
            def _():
                hidden(b, c, to).wait_recv()

            @pl.when((e != end) & (e != begin))
            def _():
                hidden(b, c, back).start()

    for b, down in order:
        combine(b, down)

    load_out.wait()
    wide = 256 if width % 256 == 0 else width

    def stage_d(k):
        es = order[k][0]
        relay(*order[k])
        second = signs(es) < 0
        h = jnp.concatenate([hid[es, c] for c in range(tiles)], axis=-1).astype(jnp.float32)
        h0 = jnp.where(second, 0.0, h).astype(jnp.bfloat16)
        h1 = jnp.where(second, h, 0.0).astype(jnp.bfloat16)

        def column(i):
            if wide == width:
                cols = slice(None)
            else:
                cols = pl.ds(pl.multiple_of(i * wide, wide), wide)
            value = jnp.dot(h0, wo[0, :, cols], preferred_element_type=jnp.float32)
            value = value + jnp.dot(h1, wo[1, :, cols], preferred_element_type=jnp.float32)
            value = value.astype(jnp.bfloat16).reshape(2, n_t, rows, wide)
            o_both[es, :, :, :, cols] = value

        if wide == width:
            column(0)
        else:
            lax.fori_loop(0, width // wide, lambda i, c: (column(i), c)[1], 0)
        sibling(es).start()

    def stage_e(k):
        es = order[k][0]
        sibling(es).wait_recv()
        both = o_both[es, p].astype(jnp.float32) + o_sib[es].astype(jnp.float32)
        x_out[es] = both.astype(jnp.bfloat16)
        for i in range(1, n_t):
            reduce_x(es, lax.rem(t + i, n_t), t).start()

    def stage_f(k):
        es = order[k][0]
        value = x_out[es, t].astype(jnp.float32)
        for i in range(1, n_t):
            ts = lax.rem(t + i, n_t)
            reduce_x(es, ts, ts).wait_recv()
            value = value + x_in[es, ts].astype(jnp.float32)
        value = value.astype(jnp.bfloat16)

        @pl.when(e == es)
        def _():
            z_in[es] = value

        @pl.when(e != es)
        def _():
            z_out[es] = value
            deliver(es, e).start()

    for step in range(n_z + 2):
        if step < n_z:
            stage_d(step)
        if 0 <= step - 1 < n_z:
            stage_e(step - 1)
        if 0 <= step - 2 < n_z:
            stage_f(step - 2)

    for k in range(n_z):
        es = lax.rem(e + k, n_z)
        if k > 0:
            deliver(es, es).wait_recv()
        owner = es // n_r
        j = lax.rem(es, n_r)

        @pl.when(owner != t)
        def _():
            finish(es, owner, j, t).start()

        @pl.when(owner == t)
        def _():
            last[j, t] = z_in[es]

    for k in range(1, n_t):
        ts = lax.rem(t + k, n_t)
        for j in range(n_r):
            finish(0, ts, j, ts).wait_recv()
    out_ref[...] = last[...]

    for k in range(1, n_t):
        ts = lax.rem(t + k, n_t)
        for j in range(n_r):
            spread(ts, j, t).wait_send()
            finish(ts * n_r + j, ts, j, t).wait_send()
        for b in range(n_z):
            widen(b, ts, t).wait_send()
            reduce_x(b, ts, t).wait_send()
    for k in range(1, n_z):
        es = lax.rem(e + k, n_z)
        across(es, es, e).wait_send()
        deliver(es, e).wait_send()
    for b in range(n_z):
        pair(b, p).wait_send()
        sibling(b).wait_send()
    for b, down in order:
        begin, end = (last_z, 0) if down else (0, last_z)
        to, back = (prev_z, next_z) if down else (next_z, prev_z)

        @pl.when(e != end)
        def _():
            for c in range(2 * tiles):
                partial(b, c, to).wait_send()

        @pl.when(e != begin)
        def _():
            for c in range(tiles):
                hidden(b, c, back).wait_send()


def local(
    tokens, route_weight, block_start, block_count, spill_rows, spill_count, in_weights, out_weights
):
    rows_each, cols = tokens.shape
    n_z = lax.axis_size("expert")
    n_t = lax.axis_size("tensor")
    n_r = n_z // n_t
    width = in_weights.shape[1]
    half = in_weights.shape[3]
    scales = token_scales(
        route_weight, block_start[0], block_count[0], spill_rows[0], spill_count[0]
    )
    signed = (scales[0] - scales[1]).astype(jnp.bfloat16)
    rows = -(-rows_each // (16 * n_t)) * 16
    extra = rows * n_t - rows_each
    if extra:
        tokens = jnp.pad(tokens, ((0, extra), (0, 0)))
        signed = jnp.pad(signed, (0, extra))
    meta = jnp.broadcast_to(signed.reshape(n_t, 1, rows, 1), (n_t, n_r, rows, LANES))
    blocks = tokens.reshape(n_t, rows, n_r, width).transpose(0, 2, 1, 3)
    xs = jnp.concatenate([meta, blocks], axis=-1)
    w_in = in_weights.transpose(0, 2, 1, 3)

    total = 2 * n_t * rows
    long = width + LANES
    tile = min(half, 256)
    tiles = half // tile
    b16 = jnp.bfloat16
    dma = pltpu.SemaphoreType.DMA
    sems = [
        dma((2,)), dma((2,)),
        dma((n_t, n_r)), dma((n_t, n_r)),
        dma((n_z,)), dma((n_z,)),
        dma((n_z, n_t)), dma((n_z, n_t)),
        dma((n_z,)), dma((n_z,)),
        dma((n_z, 2 * tiles)), dma((n_z, 2 * tiles)),
        dma((n_z, tiles)), dma((n_z, tiles)),
        dma((n_z,)), dma((n_z,)),
        dma((n_z, n_t)), dma((n_z, n_t)),
        dma((n_z,)), dma((n_z,)),
        dma((n_z,)), dma((n_r, n_t)),
    ]
    vmem = pltpu.VMEM
    out = pl.pallas_call(
        functools.partial(kernel, n_t, n_z, n_r, rows, width, half),
        out_shape=jax.ShapeDtypeStruct((n_r, n_t, rows, width), b16),
        in_specs=[
            pl.BlockSpec(memory_space=pltpu.VMEM),
            pl.BlockSpec(memory_space=pl.ANY),
            pl.BlockSpec(memory_space=pl.ANY),
        ],
        out_specs=pl.BlockSpec(memory_space=pltpu.VMEM),
        scratch_shapes=[
            vmem(w_in.shape, b16),
            vmem(out_weights.shape, b16),
            vmem((n_t, n_r, rows, long), b16),
            vmem((n_z, 2, n_t, rows, long), b16),
            vmem((n_z, 2 * tiles, total, tile), jnp.float32),
            vmem((n_z, 2 * tiles, total, tile), b16),
            vmem((n_z, 2 * tiles, total, tile), b16),
            vmem((n_z, tiles, total, tile), b16),
            vmem((n_z, 2, n_t, rows, width), b16),
            vmem((n_z, n_t, rows, width), b16),
            vmem((n_z, n_t, rows, width), b16),
            vmem((n_z, n_t, rows, width), b16),
            vmem((n_z, rows, width), b16),
            vmem((n_z, rows, width), b16),
            vmem((n_r, n_t, rows, width), b16),
        ] + sems,
        compiler_params=pltpu.CompilerParams(
            collective_id=0, has_side_effects=True, vmem_limit_bytes=56 * 1024 * 1024
        ),
    )(xs, w_in, out_weights)
    out = out.transpose(1, 2, 0, 3).reshape(n_t * rows, cols)
    return out[:rows_each]


def solution(mesh):
    return jax.shard_map(
        local,
        mesh=mesh,
        in_specs=(
            P(("groups", "expert", "dp"), "tensor"),
            P(("groups", "expert", "dp")),
            P(("groups", "expert", "dp"), None),
            P(("groups", "expert", "dp"), None),
            P(("groups", "expert", "dp"), None, None),
            P(("groups", "expert", "dp"), None),
            P(None, "expert", None, ("tensor", "dp")),
            P(None, ("tensor", "dp"), "expert"),
        ),
        out_specs=P(("groups", "expert", "dp"), "tensor"),
        check_vma=False,
    )
```

```python
import functools

import jax
import jax.numpy as jnp
from jax import lax
from jax.experimental import pallas as pl
from jax.experimental.pallas import tpu as pltpu
from jax.sharding import PartitionSpec as P

MESH = pl.DeviceIdType.MESH
LANES = 128


def signed_scales(count_rows, padded, weight, starts, counts, spills, spill_counts):
    overflow = spills.shape[-1]
    capacity = count_rows - overflow
    sums = []
    for ex in range(2):
        row = lax.broadcasted_iota(jnp.int32, (padded, capacity), 0)
        pos = lax.broadcasted_iota(jnp.int32, (padded, capacity), 1)
        slot = jnp.clip(starts[:, ex : ex + 1] + pos, 0, count_rows - 1)
        hit = jnp.where((slot == row) & (pos < counts[:, ex : ex + 1]), 1.0, 0.0)
        row = lax.broadcasted_iota(jnp.int32, (padded, overflow), 0)
        pos = lax.broadcasted_iota(jnp.int32, (padded, overflow), 1)
        slot = jnp.clip(spills[ex : ex + 1, :], 0, count_rows - 1)
        more = jnp.where((slot == row) & (pos < spill_counts[:, ex : ex + 1]), 1.0, 0.0)
        sums.append(
            jnp.sum(hit, axis=1, keepdims=True) + jnp.sum(more, axis=1, keepdims=True)
        )
    row = lax.broadcasted_iota(jnp.int32, (padded, padded), 0)
    col = lax.broadcasted_iota(jnp.int32, (padded, padded), 1)
    weight = jnp.broadcast_to(weight.astype(jnp.float32), (padded, padded))
    column = jnp.sum(jnp.where(row == col, weight, 0.0), axis=1, keepdims=True)
    return (sums[0] - sums[1]) * column


def kernel(
    n_t, n_z, n_r, rows, width, half, rows_each,
    tokens, weight, starts, counts, spills, spill_counts, w_in, w_out, out_ref,
    xs, wi, wo, first, x_all, part, run_out, run_in, hid, o_both, o_sib, x_out, x_in, z_out, z_in, last,
    wsem, lsem, s0, r0, s1, r1, s2, r2, s3, r3, s4, r4, s5, r5, s6, r6, s7, r7, s8, r8, s9, r9,
):
    e = lax.axis_index("expert")
    t = lax.axis_index("tensor")
    p = lax.axis_index("dp")
    other = 1 - p
    total = 2 * n_t * rows

    load_in = pltpu.make_async_copy(w_in, wi, wsem.at[0])
    load_out = pltpu.make_async_copy(w_out, wo, wsem.at[1])
    own_piece = pltpu.make_async_copy(xs.at[t], first.at[t], lsem.at[0])
    load_in.start()
    load_out.start()

    barrier = pltpu.get_barrier_semaphore()
    for k in range(1, n_t):
        pl.semaphore_signal(
            barrier, inc=1, device_id={"tensor": lax.rem(t + k, n_t)}, device_id_type=MESH
        )
    for k in range(1, n_z):
        pl.semaphore_signal(
            barrier, inc=1, device_id={"expert": lax.rem(e + k, n_z)}, device_id_type=MESH
        )
    pl.semaphore_signal(barrier, inc=1, device_id={"dp": other}, device_id_type=MESH)
    signed = signed_scales(
        rows_each, n_t * rows, weight[...], starts[...], counts[...], spills[...], spill_counts[...]
    )
    meta = jnp.broadcast_to(signed, (n_t * rows, LANES)).astype(jnp.bfloat16)
    for i in range(n_t):
        piece = slice(i * rows, (i + 1) * rows)
        for j in range(n_r):
            xs[i, j, :, :LANES] = meta[piece]
            xs[i, j, :, LANES:] = tokens[piece, j * width : (j + 1) * width]
    own_piece.start()
    pl.semaphore_wait(barrier, n_t + n_z - 1)

    def remote(src, dst, send, recv, **where):
        return pltpu.make_async_remote_copy(
            src_ref=src,
            dst_ref=dst,
            send_sem=send,
            recv_sem=recv,
            device_id=where,
            device_id_type=MESH,
        )

    def spread(to, j, came):
        return remote(
            xs.at[to, j], first.at[came, j], s0.at[to, j], r0.at[came, j], tensor=to
        )

    def across(block, to, came):
        return remote(
            first.at[block // n_r, lax.rem(block, n_r)],
            x_all.at[came, p, t],
            s1.at[to],
            r1.at[came],
            expert=to,
        )

    def widen(block, to, came):
        return remote(
            x_all.at[block, p, came],
            x_all.at[block, p, came],
            s2.at[block, to],
            r2.at[block, came],
            tensor=to,
        )

    def pair(block, core):
        return remote(
            x_all.at[block, core], x_all.at[block, core], s3.at[block], r3.at[block], dp=other
        )

    def partial(block, c, to):
        return remote(
            run_out.at[block, c], run_in.at[block, c], s4.at[block, c], r4.at[block, c], expert=to
        )

    def hidden(block, c, to):
        return remote(
            hid.at[block, c], hid.at[block, c], s5.at[block, c], r5.at[block, c], expert=to
        )

    last_z = n_z - 1
    order = []
    for i in range(n_z // 2):
        order += [(last_z - i, True), (i, False)]
    prev_z = jnp.maximum(e - 1, 0)
    next_z = jnp.minimum(e + 1, last_z)

    def sibling(block):
        return remote(
            o_both.at[block, other], o_sib.at[block], s6.at[block], r6.at[block], dp=other
        )

    def reduce_x(block, to, came):
        return remote(
            x_out.at[block, to], x_in.at[block, came], s7.at[block, to], r7.at[block, came],
            tensor=to,
        )

    def deliver(to, came):
        return remote(z_out.at[to], z_in.at[came], s8.at[to], r8.at[came], expert=to)

    def finish(block, to, j, came):
        return remote(
            z_in.at[block], last.at[j, came], s9.at[block], r9.at[j, came], tensor=to
        )

    for j in range(n_r):
        for k in range(1, n_t):
            spread(lax.rem(t + k, n_t), j, t).start()
    own_piece.wait()
    for k in range(n_t):
        ts = lax.rem(t + k, n_t)
        for j in range(n_r):
            block = ts * n_r + j
            if k > 0:
                spread(ts, j, ts).wait_recv()

            @pl.when(block != e)
            def _():
                across(block, block, e).start()

            @pl.when(block == e)
            def _():
                pltpu.make_async_copy(first.at[ts, j], x_all.at[e, p, t], lsem.at[1]).start()

    def stage_a(k):
        es = lax.rem(e + k, n_z)
        if k == 0:
            pltpu.make_async_copy(first.at[0, 0], x_all.at[e, p, t], lsem.at[1]).wait()
        else:
            across(es, es, es).wait_recv()
        for i in range(1, n_t):
            widen(es, lax.rem(t + i, n_t), t).start()

    def stage_b(k):
        es = lax.rem(e + k, n_z)
        for i in range(1, n_t):
            ts = lax.rem(t + i, n_t)
            widen(es, ts, ts).wait_recv()
        pair(es, p).start()

    def signs(es):
        meta = x_all[es, :, :, :, :LANES].reshape(total, LANES)
        return meta.astype(jnp.float32)[:, :1]

    tile = min(half, 256)
    tiles = half // tile

    def stage_c(k):
        es = lax.rem(e + k, n_z)
        pair(es, other).wait_recv()
        second = signs(es) < 0

        def step(i, carry):
            g = i // tiles
            cols = pl.ds(pl.multiple_of(lax.rem(i, tiles) * tile, tile), tile)
            x = x_all[es, :, :, :, LANES:].reshape(total, width)
            zero = jnp.dot(x, wi[0, g, :, cols], preferred_element_type=jnp.float32)
            one = jnp.dot(x, wi[1, g, :, cols], preferred_element_type=jnp.float32)
            part[es, i] = jnp.where(second, one, zero)
            return carry

        lax.fori_loop(0, 2 * tiles, step, 0)

        @pl.when((e == last_z) & (es >= n_z // 2))
        def _():
            for c in range(2 * tiles):
                run_out[es, c] = part[es, c].astype(jnp.bfloat16)
                partial(es, c, prev_z).start()

        @pl.when((e == 0) & (es < n_z // 2))
        def _():
            for c in range(2 * tiles):
                run_out[es, c] = part[es, c].astype(jnp.bfloat16)
                partial(es, c, next_z).start()

    for step in range(n_z + 2):
        if step < n_z:
            stage_a(step)
        if 0 <= step - 1 < n_z:
            stage_b(step - 1)
        if step - 1 == 0:
            load_in.wait()
        if 0 <= step - 2 < n_z:
            stage_c(step - 2)

    def combine(b, down):
        begin, end = (last_z, 0) if down else (0, last_z)
        to, back = (prev_z, next_z) if down else (next_z, prev_z)

        @pl.when((e != begin) & (e != end))
        def _():
            for c in range(2 * tiles):
                partial(b, c, back).wait_recv()
                value = part[b, c] + run_in[b, c].astype(jnp.float32)
                run_out[b, c] = value.astype(jnp.bfloat16)
                partial(b, c, to).start()

        @pl.when(e == end)
        def _():
            for c in range(2 * tiles):
                partial(b, c, back).wait_recv()
            scale = jnp.abs(signs(b))
            for c in range(tiles):
                gate = part[b, c] + run_in[b, c].astype(jnp.float32)
                up = part[b, tiles + c] + run_in[b, tiles + c].astype(jnp.float32)
                act = gate / (1.0 + jnp.exp(-gate)) * up * scale
                hid[b, c] = act.astype(jnp.bfloat16)
                hidden(b, c, back).start()

    def relay(b, down):
        begin, end = (last_z, 0) if down else (0, last_z)
        to, back = (prev_z, next_z) if down else (next_z, prev_z)
        for c in range(tiles):

            @pl.when(e != end)
            def _():
                hidden(b, c, to).wait_recv()

            @pl.when((e != end) & (e != begin))
            def _():
                hidden(b, c, back).start()

    for b, down in order:
        combine(b, down)

    load_out.wait()
    wide = 256 if width % 256 == 0 else width

    def stage_d(k):
        es = order[k][0]
        second = signs(es) < 0
        h = jnp.concatenate([hid[es, c] for c in range(tiles)], axis=-1).astype(jnp.float32)
        h0 = jnp.where(second, 0.0, h).astype(jnp.bfloat16)
        h1 = jnp.where(second, h, 0.0).astype(jnp.bfloat16)

        def column(i):
            if wide == width:
                cols = slice(None)
            else:
                cols = pl.ds(pl.multiple_of(i * wide, wide), wide)
            value = jnp.dot(h0, wo[0, :, cols], preferred_element_type=jnp.float32)
            value = value + jnp.dot(h1, wo[1, :, cols], preferred_element_type=jnp.float32)
            value = value.astype(jnp.bfloat16).reshape(2, n_t, rows, wide)
            o_both[es, :, :, :, cols] = value

        if wide == width:
            column(0)
        else:
            lax.fori_loop(0, width // wide, lambda i, c: (column(i), c)[1], 0)
        sibling(es).start()

    def stage_e(k):
        es = order[k][0]
        sibling(es).wait_recv()
        both = o_both[es, p].astype(jnp.float32) + o_sib[es].astype(jnp.float32)
        x_out[es] = both.astype(jnp.bfloat16)
        for i in range(1, n_t):
            reduce_x(es, lax.rem(t + i, n_t), t).start()

    def stage_f(k):
        es = order[k][0]
        value = x_out[es, t].astype(jnp.float32)
        for i in range(1, n_t):
            ts = lax.rem(t + i, n_t)
            reduce_x(es, ts, ts).wait_recv()
            value = value + x_in[es, ts].astype(jnp.float32)
        value = value.astype(jnp.bfloat16)

        @pl.when(e == es)
        def _():
            z_in[es] = value

        @pl.when(e != es)
        def _():
            z_out[es] = value
            deliver(es, e).start()

    for step in range(n_z + 2):
        if step > 0 and step % 2 == 0 and step - 1 < n_z:
            stage_e(step - 1)
        if step < n_z:
            if step == 0:
                for b, down in order:
                    relay(b, down)
            stage_d(step)
        if 0 <= step - 1 < n_z and step % 2 == 1:
            stage_e(step - 1)
        if 0 <= step - 2 < n_z:
            stage_f(step - 2)

    for k in range(n_z):
        es = lax.rem(e + k, n_z)
        if k > 0:
            deliver(es, es).wait_recv()
        owner = es // n_r
        j = lax.rem(es, n_r)

        @pl.when(owner != t)
        def _():
            finish(es, owner, j, t).start()

        @pl.when(owner == t)
        def _():
            last[j, t] = z_in[es]

    for k in range(1, n_t):
        ts = lax.rem(t + k, n_t)
        for j in range(n_r):
            finish(0, ts, j, ts).wait_recv()
    for i in range(n_t):
        for j in range(n_r):
            out_ref[i * rows : (i + 1) * rows, j * width : (j + 1) * width] = last[j, i]

    for k in range(1, n_t):
        ts = lax.rem(t + k, n_t)
        for j in range(n_r):
            spread(ts, j, t).wait_send()
            finish(ts * n_r + j, ts, j, t).wait_send()
        for b in range(n_z):
            widen(b, ts, t).wait_send()
            reduce_x(b, ts, t).wait_send()
    for k in range(1, n_z):
        es = lax.rem(e + k, n_z)
        across(es, es, e).wait_send()
        deliver(es, e).wait_send()
    for b in range(n_z):
        pair(b, p).wait_send()
        sibling(b).wait_send()
    for b, down in order:
        begin, end = (last_z, 0) if down else (0, last_z)
        to, back = (prev_z, next_z) if down else (next_z, prev_z)

        @pl.when(e != end)
        def _():
            for c in range(2 * tiles):
                partial(b, c, to).wait_send()

        @pl.when(e != begin)
        def _():
            for c in range(tiles):
                hidden(b, c, back).wait_send()


def local(
    tokens, route_weight, block_start, block_count, spill_rows, spill_count, in_weights, out_weights
):
    rows_each, cols = tokens.shape
    n_z = lax.axis_size("expert")
    n_t = lax.axis_size("tensor")
    n_r = n_z // n_t
    width = in_weights.shape[1]
    half = in_weights.shape[3]
    rows = -(-rows_each // (16 * n_t)) * 16
    extra = rows * n_t - rows_each
    if extra:
        tokens = jnp.pad(tokens, ((0, extra), (0, 0)))
        route_weight = jnp.pad(route_weight, (0, extra))
    w_in = in_weights.transpose(0, 2, 1, 3)

    total = 2 * n_t * rows
    long = width + LANES
    tile = min(half, 256)
    tiles = half // tile
    b16 = jnp.bfloat16
    dma = pltpu.SemaphoreType.DMA
    sems = [
        dma((2,)), dma((2,)),
        dma((n_t, n_r)), dma((n_t, n_r)),
        dma((n_z,)), dma((n_z,)),
        dma((n_z, n_t)), dma((n_z, n_t)),
        dma((n_z,)), dma((n_z,)),
        dma((n_z, 2 * tiles)), dma((n_z, 2 * tiles)),
        dma((n_z, tiles)), dma((n_z, tiles)),
        dma((n_z,)), dma((n_z,)),
        dma((n_z, n_t)), dma((n_z, n_t)),
        dma((n_z,)), dma((n_z,)),
        dma((n_z,)), dma((n_r, n_t)),
    ]
    vmem = pltpu.VMEM
    out = pl.pallas_call(
        functools.partial(kernel, n_t, n_z, n_r, rows, width, half, rows_each),
        out_shape=jax.ShapeDtypeStruct((n_t * rows, cols), b16),
        in_specs=[
            pl.BlockSpec(memory_space=pltpu.VMEM),
            pl.BlockSpec(memory_space=pltpu.VMEM),
            pl.BlockSpec(memory_space=pltpu.VMEM),
            pl.BlockSpec(memory_space=pltpu.VMEM),
            pl.BlockSpec(memory_space=pltpu.VMEM),
            pl.BlockSpec(memory_space=pltpu.VMEM),
            pl.BlockSpec(memory_space=pl.ANY),
            pl.BlockSpec(memory_space=pl.ANY),
        ],
        out_specs=pl.BlockSpec(memory_space=pltpu.VMEM),
        scratch_shapes=[
            vmem((n_t, n_r, rows, long), b16),
            vmem(w_in.shape, b16),
            vmem(out_weights.shape, b16),
            vmem((n_t, n_r, rows, long), b16),
            vmem((n_z, 2, n_t, rows, long), b16),
            vmem((n_z, 2 * tiles, total, tile), jnp.float32),
            vmem((n_z, 2 * tiles, total, tile), b16),
            vmem((n_z, 2 * tiles, total, tile), b16),
            vmem((n_z, tiles, total, tile), b16),
            vmem((n_z, 2, n_t, rows, width), b16),
            vmem((n_z, n_t, rows, width), b16),
            vmem((n_z, n_t, rows, width), b16),
            vmem((n_z, n_t, rows, width), b16),
            vmem((n_z, rows, width), b16),
            vmem((n_z, rows, width), b16),
            vmem((n_r, n_t, rows, width), b16),
        ] + sems,
        compiler_params=pltpu.CompilerParams(
            collective_id=0, has_side_effects=True, vmem_limit_bytes=56 * 1024 * 1024
        ),
    )(
        tokens,
        route_weight[None],
        block_start,
        block_count,
        spill_rows[0],
        spill_count,
        w_in,
        out_weights,
    )
    return out[:rows_each]


def solution(mesh):
    return jax.shard_map(
        local,
        mesh=mesh,
        in_specs=(
            P(("groups", "expert", "dp"), "tensor"),
            P(("groups", "expert", "dp")),
            P(("groups", "expert", "dp"), None),
            P(("groups", "expert", "dp"), None),
            P(("groups", "expert", "dp"), None, None),
            P(("groups", "expert", "dp"), None),
            P(None, "expert", None, ("tensor", "dp")),
            P(None, ("tensor", "dp"), "expert"),
        ),
        out_specs=P(("groups", "expert", "dp"), "tensor"),
        check_vma=False,
    )
```

```python
import functools

import jax
import jax.numpy as jnp
from jax import lax
from jax.experimental import pallas as pl
from jax.experimental.pallas import tpu as pltpu
from jax.sharding import PartitionSpec as P

MESH = pl.DeviceIdType.MESH
LANES = 128


def signed_scales(count_rows, padded, weight, starts, counts, spills, spill_counts):
    overflow = spills.shape[-1]
    capacity = count_rows - overflow
    sums = []
    for ex in range(2):
        row = lax.broadcasted_iota(jnp.int32, (padded, capacity), 0)
        pos = lax.broadcasted_iota(jnp.int32, (padded, capacity), 1)
        slot = jnp.clip(starts[:, ex : ex + 1] + pos, 0, count_rows - 1)
        hit = jnp.where((slot == row) & (pos < counts[:, ex : ex + 1]), 1.0, 0.0)
        row = lax.broadcasted_iota(jnp.int32, (padded, overflow), 0)
        pos = lax.broadcasted_iota(jnp.int32, (padded, overflow), 1)
        slot = jnp.clip(spills[ex : ex + 1, :], 0, count_rows - 1)
        more = jnp.where((slot == row) & (pos < spill_counts[:, ex : ex + 1]), 1.0, 0.0)
        sums.append(
            jnp.sum(hit, axis=1, keepdims=True) + jnp.sum(more, axis=1, keepdims=True)
        )
    row = lax.broadcasted_iota(jnp.int32, (padded, padded), 0)
    col = lax.broadcasted_iota(jnp.int32, (padded, padded), 1)
    weight = jnp.broadcast_to(weight.astype(jnp.float32), (padded, padded))
    column = jnp.sum(jnp.where(row == col, weight, 0.0), axis=1, keepdims=True)
    return (sums[0] - sums[1]) * column


def kernel(
    n_t, n_z, n_r, rows, width, half, rows_each,
    tokens, weight, starts, counts, spills, spill_counts, w_in, w_out, out_ref,
    xs, wi, wo, first, x_all, part, run_out, run_in, hid, o_both, o_sib, x_out, x_in, z_out, z_in, last,
    wsem, lsem, s0, r0, s1, r1, s2, r2, s3, r3, s4, r4, s5, r5, s6, r6, s7, r7, s8, r8, s9, r9,
):
    e = lax.axis_index("expert")
    t = lax.axis_index("tensor")
    p = lax.axis_index("dp")
    other = 1 - p
    total = 2 * n_t * rows

    load_in = pltpu.make_async_copy(w_in, wi, wsem.at[0])
    load_out = pltpu.make_async_copy(w_out, wo, wsem.at[1])
    own_piece = pltpu.make_async_copy(xs.at[t], first.at[t], lsem.at[0])
    load_in.start()
    load_out.start()

    barrier = pltpu.get_barrier_semaphore()
    for k in range(1, n_t):
        pl.semaphore_signal(
            barrier, inc=1, device_id={"tensor": lax.rem(t + k, n_t)}, device_id_type=MESH
        )
    for k in range(1, n_z):
        pl.semaphore_signal(
            barrier, inc=1, device_id={"expert": lax.rem(e + k, n_z)}, device_id_type=MESH
        )
    pl.semaphore_signal(barrier, inc=1, device_id={"dp": other}, device_id_type=MESH)
    signed = signed_scales(
        rows_each, n_t * rows, weight[...], starts[...], counts[...], spills[...], spill_counts[...]
    )
    meta = jnp.broadcast_to(signed, (n_t * rows, LANES)).astype(jnp.bfloat16)
    for i in range(n_t):
        piece = slice(i * rows, (i + 1) * rows)
        for j in range(n_r):
            xs[i, j, :, :LANES] = meta[piece]
            xs[i, j, :, LANES:] = tokens[piece, j * width : (j + 1) * width]
    own_piece.start()
    pl.semaphore_wait(barrier, n_t + n_z - 1)

    def remote(src, dst, send, recv, **where):
        return pltpu.make_async_remote_copy(
            src_ref=src,
            dst_ref=dst,
            send_sem=send,
            recv_sem=recv,
            device_id=where,
            device_id_type=MESH,
        )

    def spread(to, j, came):
        return remote(
            xs.at[to, j], first.at[came, j], s0.at[to, j], r0.at[came, j], tensor=to
        )

    def across(block, to, came):
        return remote(
            first.at[block // n_r, lax.rem(block, n_r)],
            x_all.at[came, p, t],
            s1.at[to],
            r1.at[came],
            expert=to,
        )

    def widen(block, to, came):
        return remote(
            x_all.at[block, p, came],
            x_all.at[block, p, came],
            s2.at[block, to],
            r2.at[block, came],
            tensor=to,
        )

    def pair(block, core):
        return remote(
            x_all.at[block, core], x_all.at[block, core], s3.at[block], r3.at[block], dp=other
        )

    def partial(block, c, to):
        return remote(
            run_out.at[block, c], run_in.at[block, c], s4.at[block, c], r4.at[block, c], expert=to
        )

    def hidden(block, c, to):
        return remote(
            hid.at[block, c], hid.at[block, c], s5.at[block, c], r5.at[block, c], expert=to
        )

    last_z = n_z - 1
    order = []
    for i in range(n_z // 2):
        order += [(last_z - i, True), (i, False)]
    prev_z = jnp.maximum(e - 1, 0)
    next_z = jnp.minimum(e + 1, last_z)

    def sibling(block):
        return remote(
            o_both.at[block, other], o_sib.at[block], s6.at[block], r6.at[block], dp=other
        )

    def reduce_x(block, to, came):
        return remote(
            x_out.at[block, to], x_in.at[block, came], s7.at[block, to], r7.at[block, came],
            tensor=to,
        )

    def deliver(to, came):
        return remote(z_out.at[to], z_in.at[came], s8.at[to], r8.at[came], expert=to)

    def finish(block, to, j, came):
        return remote(
            z_in.at[block], last.at[j, came], s9.at[block], r9.at[j, came], tensor=to
        )

    for j in range(n_r):
        for k in range(1, n_t):
            spread(lax.rem(t + k, n_t), j, t).start()
    own_piece.wait()
    for k in range(n_t):
        ts = lax.rem(t + k, n_t)
        for j in range(n_r):
            block = ts * n_r + j
            if k > 0:
                spread(ts, j, ts).wait_recv()

            @pl.when(block != e)
            def _():
                across(block, block, e).start()

            @pl.when(block == e)
            def _():
                pltpu.make_async_copy(first.at[ts, j], x_all.at[e, p, t], lsem.at[1]).start()

    def stage_a(k):
        es = lax.rem(e + k, n_z)
        if k == 0:
            pltpu.make_async_copy(first.at[0, 0], x_all.at[e, p, t], lsem.at[1]).wait()
        else:
            across(es, es, es).wait_recv()
        for i in range(1, n_t):
            widen(es, lax.rem(t + i, n_t), t).start()

    def stage_b(k):
        es = lax.rem(e + k, n_z)
        for i in range(1, n_t):
            ts = lax.rem(t + i, n_t)
            widen(es, ts, ts).wait_recv()
        pair(es, p).start()

    def signs(es):
        meta = x_all[es, :, :, :, :LANES].reshape(total, LANES)
        return meta.astype(jnp.float32)[:, :1]

    tile = min(half, 256)
    tiles = half // tile

    def stage_c(k):
        es = lax.rem(e + k, n_z)
        pair(es, other).wait_recv()
        second = signs(es) < 0

        def step(i, carry):
            g = i // tiles
            cols = pl.ds(pl.multiple_of(lax.rem(i, tiles) * tile, tile), tile)
            x = x_all[es, :, :, :, LANES:].reshape(total, width)
            zero = jnp.dot(x, wi[0, g, :, cols], preferred_element_type=jnp.float32)
            one = jnp.dot(x, wi[1, g, :, cols], preferred_element_type=jnp.float32)
            part[es, i] = jnp.where(second, one, zero)
            return carry

        lax.fori_loop(0, 2 * tiles, step, 0)

        @pl.when((e == last_z) & (es >= n_z // 2))
        def _():
            for c in range(2 * tiles):
                run_out[es, c] = part[es, c].astype(jnp.bfloat16)
                partial(es, c, prev_z).start()

        @pl.when((e == 0) & (es < n_z // 2))
        def _():
            for c in range(2 * tiles):
                run_out[es, c] = part[es, c].astype(jnp.bfloat16)
                partial(es, c, next_z).start()

    for step in range(n_z + 2):
        if step < n_z:
            stage_a(step)
        if 0 <= step - 1 < n_z:
            stage_b(step - 1)
        if step - 1 == 0:
            load_in.wait()
        if 0 <= step - 2 < n_z:
            stage_c(step - 2)

    def combine(b, down):
        begin, end = (last_z, 0) if down else (0, last_z)
        to, back = (prev_z, next_z) if down else (next_z, prev_z)

        @pl.when((e != begin) & (e != end))
        def _():
            for c in range(2 * tiles):
                partial(b, c, back).wait_recv()
                value = part[b, c] + run_in[b, c].astype(jnp.float32)
                run_out[b, c] = value.astype(jnp.bfloat16)
                partial(b, c, to).start()

        @pl.when(e == end)
        def _():
            for c in range(2 * tiles):
                partial(b, c, back).wait_recv()
            scale = jnp.abs(signs(b))
            for c in range(tiles):
                gate = part[b, c] + run_in[b, c].astype(jnp.float32)
                up = part[b, tiles + c] + run_in[b, tiles + c].astype(jnp.float32)
                act = gate / (1.0 + jnp.exp(-gate)) * up * scale
                hid[b, c] = act.astype(jnp.bfloat16)
                hidden(b, c, back).start()

    def relay(b, down):
        begin, end = (last_z, 0) if down else (0, last_z)
        to, back = (prev_z, next_z) if down else (next_z, prev_z)
        for c in range(tiles):

            @pl.when(e != end)
            def _():
                hidden(b, c, to).wait_recv()

            @pl.when((e != end) & (e != begin))
            def _():
                hidden(b, c, back).start()

    for b, down in order:
        combine(b, down)

    load_out.wait()
    wide = 256 if width % 256 == 0 else width

    def stage_d(k):
        es = order[k][0]
        second = signs(es) < 0
        h = jnp.concatenate([hid[es, c] for c in range(tiles)], axis=-1).astype(jnp.float32)
        h0 = jnp.where(second, 0.0, h).astype(jnp.bfloat16)
        h1 = jnp.where(second, h, 0.0).astype(jnp.bfloat16)

        def column(i):
            if wide == width:
                cols = slice(None)
            else:
                cols = pl.ds(pl.multiple_of(i * wide, wide), wide)
            value = jnp.dot(h0, wo[0, :, cols], preferred_element_type=jnp.float32)
            value = value + jnp.dot(h1, wo[1, :, cols], preferred_element_type=jnp.float32)
            value = value.astype(jnp.bfloat16).reshape(2, n_t, rows, wide)
            o_both[es, :, :, :, cols] = value

        if wide == width:
            column(0)
        else:
            lax.fori_loop(0, width // wide, lambda i, c: (column(i), c)[1], 0)
        sibling(es).start()

    def stage_e(k):
        es = order[k][0]
        sibling(es).wait_recv()
        both = o_both[es, p].astype(jnp.float32) + o_sib[es].astype(jnp.float32)
        x_out[es] = both.astype(jnp.bfloat16)
        for i in range(1, n_t):
            reduce_x(es, lax.rem(t + i, n_t), t).start()

    def stage_f(k):
        es = order[k][0]
        value = x_out[es, t].astype(jnp.float32)
        for i in range(1, n_t):
            ts = lax.rem(t + i, n_t)
            reduce_x(es, ts, ts).wait_recv()
            value = value + x_in[es, ts].astype(jnp.float32)
        value = value.astype(jnp.bfloat16)

        @pl.when(e == es)
        def _():
            z_in[es] = value

        @pl.when(e != es)
        def _():
            z_out[es] = value
            deliver(es, e).start()

    for step in range(n_z + 2):
        if step > 0 and step % 2 == 0 and step - 1 < n_z:
            stage_e(step - 1)
        if step < n_z:
            if step == 0:
                for b, down in order:
                    relay(b, down)
            stage_d(step)
        if 0 <= step - 1 < n_z and step % 2 == 1:
            stage_e(step - 1)
        if 0 <= step - 2 < n_z:
            stage_f(step - 2)

    for k in range(n_z):
        es = lax.rem(e + k, n_z)
        if k > 0:
            deliver(es, es).wait_recv()
        owner = es // n_r
        j = lax.rem(es, n_r)

        @pl.when(owner != t)
        def _():
            finish(es, owner, j, t).start()

        @pl.when(owner == t)
        def _():
            last[j, t] = z_in[es]

    for k in range(1, n_t):
        ts = lax.rem(t + k, n_t)
        for j in range(n_r):
            finish(0, ts, j, ts).wait_recv()
    for i in range(n_t):
        for j in range(n_r):
            out_ref[i * rows : (i + 1) * rows, j * width : (j + 1) * width] = last[j, i]

    for k in range(1, n_t):
        ts = lax.rem(t + k, n_t)
        for j in range(n_r):
            spread(ts, j, t).wait_send()
            finish(ts * n_r + j, ts, j, t).wait_send()
        for b in range(n_z):
            widen(b, ts, t).wait_send()
            reduce_x(b, ts, t).wait_send()
    for k in range(1, n_z):
        es = lax.rem(e + k, n_z)
        across(es, es, e).wait_send()
        deliver(es, e).wait_send()
    for b in range(n_z):
        pair(b, p).wait_send()
        sibling(b).wait_send()
    for b, down in order:
        begin, end = (last_z, 0) if down else (0, last_z)
        to, back = (prev_z, next_z) if down else (next_z, prev_z)

        @pl.when(e != end)
        def _():
            for c in range(2 * tiles):
                partial(b, c, to).wait_send()

        @pl.when(e != begin)
        def _():
            for c in range(tiles):
                hidden(b, c, back).wait_send()


def local(
    tokens, route_weight, block_start, block_count, spill_rows, spill_count, in_weights, out_weights
):
    rows_each, cols = tokens.shape
    n_z = lax.axis_size("expert")
    n_t = lax.axis_size("tensor")
    n_r = n_z // n_t
    width = in_weights.shape[1]
    half = in_weights.shape[3]
    rows = -(-rows_each // (16 * n_t)) * 16
    extra = rows * n_t - rows_each
    if extra:
        tokens = jnp.pad(tokens, ((0, extra), (0, 0)))
        route_weight = jnp.pad(route_weight, (0, extra))
    w_in = in_weights.transpose(0, 2, 1, 3)

    total = 2 * n_t * rows
    long = width + LANES
    tile = min(half, 256)
    tiles = half // tile
    b16 = jnp.bfloat16
    dma = pltpu.SemaphoreType.DMA
    sems = [
        dma((2,)), dma((2,)),
        dma((n_t, n_r)), dma((n_t, n_r)),
        dma((n_z,)), dma((n_z,)),
        dma((n_z, n_t)), dma((n_z, n_t)),
        dma((n_z,)), dma((n_z,)),
        dma((n_z, 2 * tiles)), dma((n_z, 2 * tiles)),
        dma((n_z, tiles)), dma((n_z, tiles)),
        dma((n_z,)), dma((n_z,)),
        dma((n_z, n_t)), dma((n_z, n_t)),
        dma((n_z,)), dma((n_z,)),
        dma((n_z,)), dma((n_r, n_t)),
    ]
    vmem = pltpu.VMEM
    out = pl.pallas_call(
        functools.partial(kernel, n_t, n_z, n_r, rows, width, half, rows_each),
        out_shape=jax.ShapeDtypeStruct((n_t * rows, cols), b16),
        in_specs=[
            pl.BlockSpec(memory_space=pltpu.VMEM),
            pl.BlockSpec(memory_space=pltpu.VMEM),
            pl.BlockSpec(memory_space=pltpu.VMEM),
            pl.BlockSpec(memory_space=pltpu.VMEM),
            pl.BlockSpec(memory_space=pltpu.VMEM),
            pl.BlockSpec(memory_space=pltpu.VMEM),
            pl.BlockSpec(memory_space=pl.ANY),
            pl.BlockSpec(memory_space=pl.ANY),
        ],
        out_specs=pl.BlockSpec(memory_space=pltpu.VMEM),
        scratch_shapes=[
            vmem((n_t, n_r, rows, long), b16),
            vmem(w_in.shape, b16),
            vmem(out_weights.shape, b16),
            vmem((n_t, n_r, rows, long), b16),
            vmem((n_z, 2, n_t, rows, long), b16),
            vmem((n_z, 2 * tiles, total, tile), jnp.float32),
            vmem((n_z, 2 * tiles, total, tile), b16),
            vmem((n_z, 2 * tiles, total, tile), b16),
            vmem((n_z, tiles, total, tile), b16),
            vmem((n_z, 2, n_t, rows, width), b16),
            vmem((n_z, n_t, rows, width), b16),
            vmem((n_z, n_t, rows, width), b16),
            vmem((n_z, n_t, rows, width), b16),
            vmem((n_z, rows, width), b16),
            vmem((n_z, rows, width), b16),
            vmem((n_r, n_t, rows, width), b16),
        ] + sems,
        compiler_params=pltpu.CompilerParams(
            collective_id=0, has_side_effects=True, vmem_limit_bytes=40 * 1024 * 1024
        ),
    )(
        tokens,
        route_weight[None],
        block_start,
        block_count,
        spill_rows[0],
        spill_count,
        w_in,
        out_weights,
    )
    return out[:rows_each]


def solution(mesh):
    return jax.shard_map(
        local,
        mesh=mesh,
        in_specs=(
            P(("groups", "expert", "dp"), "tensor"),
            P(("groups", "expert", "dp")),
            P(("groups", "expert", "dp"), None),
            P(("groups", "expert", "dp"), None),
            P(("groups", "expert", "dp"), None, None),
            P(("groups", "expert", "dp"), None),
            P(None, "expert", None, ("tensor", "dp")),
            P(None, ("tensor", "dp"), "expert"),
        ),
        out_specs=P(("groups", "expert", "dp"), "tensor"),
        check_vma=False,
    )
```
